256 devices in a mesh: rep: 8 (over x, z_hi), ep: 32 (over y, z_lo, core).
Axes of the slice: x: 4, y: 4, z: 8 (z_hi: 2, z_lo: 4; z = z_hi * 4 + z_lo), core: 2. Of those that a mesh axis runs over, the one named last changes fastest.
Arguments:
- tokens: bfloat16 [5120, 7168], P('ep', 'rep'), may hold values from -6 to 6
- slot_ids: int32 [5120, 2], P('ep'), may hold values from 0 to 63, all different within a row; in each aligned block of 160 rows (0 to 159, 160 to 319, ...) at most 10 rows name the same one
- gate_weights_per_slot: float32 [5120, 2], P('ep'), may hold values from 0.1 to 1
- w_gate: bfloat16 [32, 7168, 2048], P('ep', None, 'rep'), may hold values from -0.0625 to 0.0625
- w_up: bfloat16 [32, 7168, 2048], P('ep', None, 'rep'), may hold values from -0.0625 to 0.0625
- w_down: bfloat16 [32, 2048, 7168], P('ep', 'rep'), may hold values from -0.1875 to 0.1875
Outputs:
- moe_output: bfloat16 [5120, 7168], P('ep', 'rep')
The draws below stay inside these ranges and needn't reach their ends.
Inputs may be any that keep to these rules, and one draw needn't show every extreme that they name: `slot_ids`: in each aligned block of 160 rows (the tokens of one index of ep) no slot is named by more than 10 rows, a bound that some block reaches; the 2 slots of a row differ.
All inputs are finite; a program needn't handle non-finite values.
Results may differ from the reference program's by a relative error of at most 0.017.
Values may be sent and summed in bfloat16 or wider, within the bound.
No kernel may reach another device: no remote copies, remote signals or barrier semaphores. Data moves between devices by JAX's collectives and lax.ppermute only.
A program may use at most 128 MiB of HBM per device.

```python
import math
import jax
import jax.numpy as jnp
import numpy as np
from jax import lax

D = 7168
FF = 2048
TOK_DEV = 160
TOP = 2
CAP = 10
HIDDEN_PER_SHARD = 256
EXPERTS = 32
SLOTS = 64
TOKENS = 5120
N_REP = 8
N_EP = 32


def strengthened(values, stream_key, source, target, shards_of, factor):
    owner, partner = [(jnp.arange(values.shape[position]) // (values.shape[position] // shards_of)).reshape([-1 if axis == position else 1 for axis in range(values.ndim)]) for position in (source, target)]
    chosen = jax.random.permutation(stream_key, shards_of)[partner]
    strong = (owner == chosen) | (owner == (partner + shards_of // 2) % shards_of)
    return jnp.where(strong, factor * values, values)


def block_scale(rng, shape, shards, smallest, top_value):
    def one(dim, blocks):
        steps = jax.random.uniform(jax.random.fold_in(jax.random.fold_in(rng, 6), dim), (blocks,), jnp.float32, smallest / len(shards), top_value / len(shards))
        return jnp.repeat(jnp.exp(steps), shape[dim] // blocks).reshape((-1,) + (1,) * (len(shape) - dim - 1))

    factor_of = one(*shards[0])
    for cut in shards[1:]:
        factor_of = factor_of * one(*cut)
    return factor_of


def deal_out(rng, own, number, rows, amount, top, most, slope):
    ranking = jax.random.permutation(rng, amount)
    crowded, common = load_shares(amount, rows * top, most, slope, True), load_shares(amount, rows * top, most, slope, False)
    places = jnp.arange(amount)

    def named(lengths, turn):
        used = int((lengths > 0).sum())
        fixed = max(1, used // 4)
        moved = fixed + (places - fixed + turn * (used - fixed)) % max(1, amount - fixed)
        return jnp.zeros((amount,), jnp.int32).at[ranking[jnp.where(places < fixed, places, moved)]].set(jnp.asarray(lengths, jnp.int32))

    lengths = jnp.where(number % 4 == 0, named(crowded, number // 4), named(common, number - number // 4 - 1))
    mixed = jax.random.permutation(jax.random.fold_in(own, 3), amount)
    donor, taker = mixed[0:amount // 2 * 2:2], mixed[1:amount // 2 * 2:2]
    margin = jnp.minimum(lengths[donor] - 1, most - lengths[taker]) // 2
    margin = jnp.where((donor == ranking[0]) | (taker == ranking[0]) | (lengths[taker] == 0), 0, jnp.maximum(margin, 0))
    moved = jax.random.randint(jax.random.fold_in(own, 4), (amount // 2,), 0, 1 << 20) % (margin + 1)
    lengths = lengths.at[donor].add(-moved).at[taker].add(moved)
    items = jnp.searchsorted(jnp.cumsum(lengths), jnp.arange(rows * top), side="right").astype(jnp.int32)
    grid = items.reshape(top, rows).T
    grid = grid[jax.random.permutation(jax.random.fold_in(own, 1), rows)]
    turn = jax.random.randint(jax.random.fold_in(own, 2), (rows, 1), 0, top)
    return jnp.take_along_axis(grid, (jnp.arange(top)[None, :] + turn) % top, axis=1)


def load_shares(number_of, total, bound, slope, full):
    portions = [(1 << 20) // math.isqrt(rank ** slope) + 1 for rank in range(1, number_of + 1)]
    largest = bound if full else min(bound, max(-(-total // number_of), total * portions[0] // sum(portions)))
    least = 1 if total - largest >= number_of - 1 else 0
    holding, rest = [largest] + [least] * (number_of - 1), total - largest - least * (number_of - 1)
    while rest > 0:
        candidates = [i for i in range(1, number_of) if holding[i] < largest] or [i for i in range(1, number_of) if holding[i] < bound]
        mass, remaining = sum([portions[i] for i in candidates]), rest
        for i in candidates:
            addition = min(bound - holding[i], max(1, remaining * portions[i] // mass), rest)
            holding[i] = holding[i] + addition
            rest = rest - addition
    return np.array(holding)


def gaussian(key, extent, width, bound, cuts=(), held_as=jnp.bfloat16):
    array = width * jax.random.normal(key, extent, jnp.float32)
    if cuts:
        array = array * block_scale(key, extent, cuts, -0.22, 0.18)
    return jnp.clip(array, -bound, bound).astype(held_as)


def heavy_noise(stream_key, shape, width, limit, pieces, heavy, kind=jnp.bfloat16):
    drawn = width * jax.random.normal(stream_key, shape, jnp.float32)
    if pieces:
        drawn = drawn * block_scale(stream_key, shape, pieces, -0.22, 0.18)
    return jnp.clip(strengthened(drawn, jax.random.fold_in(stream_key, 3), *heavy), -limit, limit).astype(kind)


def setup_inputs(seed: int = 0) -> dict:
    streams_of = jax.random.split(jax.random.key(seed), 7)
    tokens = gaussian(streams_of[0], (TOKENS, D), 1.0, 6.0, ((0, 32), (1, 8)))
    slot_ids_keys = jax.random.split(jax.random.fold_in(streams_of[1], 1), TOKENS // TOK_DEV)
    slot_ids_turns = jax.random.permutation(jax.random.fold_in(streams_of[1], 3), TOKENS // TOK_DEV)
    slot_ids = jax.vmap(lambda own, number: deal_out(jax.random.fold_in(streams_of[1], 2), own, number, TOK_DEV, SLOTS, TOP, CAP, 2))(slot_ids_keys, slot_ids_turns).reshape((TOKENS, TOP))
    gate_weights_per_slot = jnp.clip(0.1 + 0.9 * jax.random.uniform(streams_of[2], (TOKENS, TOP), jnp.float32) ** block_scale(streams_of[2], (TOKENS, TOP), ((0, 32),), -0.2, 0.2), 0.1, 1.0)
    w_gate = gaussian(streams_of[3], (EXPERTS, D, FF), D ** -0.5, 0.0625, ((0, 32), (2, 8)))
    w_up = gaussian(streams_of[4], (EXPERTS, D, FF), D ** -0.5, 0.0625, ((0, 32), (2, 8)))
    w_down = heavy_noise(streams_of[5], (EXPERTS, FF, D), FF ** -0.5, 0.1875, ((0, 32), (1, 8)), (1, 2, 8, 2.0))
    return dict(tokens=tokens, slot_ids=slot_ids, gate_weights_per_slot=gate_weights_per_slot, w_gate=w_gate, w_up=w_up, w_down=w_down)


def reference(tokens, slot_ids, gate_weights_per_slot, w_gate, w_up, w_down):
    flattened = slot_ids.reshape(-1)
    token_of = jnp.arange(TOKENS * TOP, dtype=jnp.int32) // TOP
    scale_flat = gate_weights_per_slot.reshape(-1)
    row_bound_count = N_EP * CAP

    def accumulate(carried, slot_now):
        device_id = slot_now // 2
        expert_id = jnp.where(slot_now % 2 == 0, device_id, (device_id - 1 + N_EP) % N_EP).astype(jnp.int32)
        ordering = jnp.argsort((flattened != slot_now).astype(jnp.int32), stable=True)[:row_bound_count]
        is_valid = flattened[ordering] == slot_now
        picked_tokens = token_of[ordering]
        inputs = tokens[picked_tokens]
        gate_mat = lax.dynamic_index_in_dim(w_gate, expert_id, 0, keepdims=False)
        up_weight_matrix = lax.dynamic_index_in_dim(w_up, expert_id, 0, keepdims=False)
        down_mat = lax.dynamic_index_in_dim(w_down, expert_id, 0, keepdims=False)
        gate_val = jnp.dot(inputs, gate_mat, preferred_element_type=jnp.float32)
        up_val = jnp.dot(inputs, up_weight_matrix, preferred_element_type=jnp.float32)
        hidden_state = (jax.nn.silu(gate_val) * up_val).astype(jnp.bfloat16)
        partial_sums = jnp.einsum("lsz,szo->slo", hidden_state.astype(jnp.float32).reshape(row_bound_count, N_REP, HIDDEN_PER_SHARD),
                              down_mat.astype(jnp.float32).reshape(N_REP, HIDDEN_PER_SHARD, D))
        rounded = lax.optimization_barrier(partial_sums.astype(jnp.bfloat16)).astype(jnp.float32)
        expert_out = jnp.sum(rounded, axis=0).astype(jnp.bfloat16)
        weights_now = jnp.where(is_valid, scale_flat[ordering], jnp.zeros_like(scale_flat[ordering]))
        carried = carried.at[picked_tokens].add(weights_now[:, None] * expert_out.astype(jnp.float32))
        return carried, None

    final_sum, unused = lax.scan(accumulate, jnp.zeros((TOKENS, D), jnp.float32), jnp.arange(SLOTS, dtype=jnp.int32))
    return final_sum.astype(jnp.bfloat16)
```

```python
import functools

import jax
import jax.numpy as jnp
from jax import lax
from jax.experimental import pallas as pl
from jax.experimental.pallas import tpu as pltpu
from jax.sharding import PartitionSpec as P

CAP_PAIR = 20
PAD_PAIR = 24
ROW_TILE = 160


def move(x, by):
    return lax.ppermute(x, "rep", [(i, (i + 2 * by) % 8) for i in range(8)])


def swap(x):
    return lax.ppermute(x, "rep", [(i, i ^ 1) for i in range(8)])


def place_rows(slot_ids, n_ep):
    flat = slot_ids.T.reshape(-1)
    count = flat.shape[0]
    onehot = (flat[:, None] == jnp.arange(2 * n_ep, dtype=jnp.int32)[None, :]).astype(jnp.bfloat16)
    before = jnp.tril(jnp.ones((count, count), jnp.bfloat16), -1)
    ahead = jnp.dot(before, onehot, preferred_element_type=jnp.float32)
    position = jnp.sum(ahead * onehot.astype(jnp.float32), axis=1).astype(jnp.int32)
    odd = flat % 2
    expert = (flat // 2 - odd + n_ep) % n_ep
    row = expert * PAD_PAIR + odd * (CAP_PAIR // 2) + position
    return row.reshape(2, -1)


def exchange(rows, n_ep):
    width = rows.shape[1]
    out = lax.all_to_all(rows.reshape(n_ep, PAD_PAIR, width), "ep", 0, 0, tiled=True)
    return out.reshape(n_ep * PAD_PAIR, width)


def compact_matrix(n_ep):
    r = lax.broadcasted_iota(jnp.int32, (n_ep * CAP_PAIR, n_ep * PAD_PAIR), 0)
    c = lax.broadcasted_iota(jnp.int32, (n_ep * CAP_PAIR, n_ep * PAD_PAIR), 1)
    return (r // CAP_PAIR * PAD_PAIR + r % CAP_PAIR == c).astype(jnp.bfloat16)


def pick(matrix, rows):
    return jnp.dot(matrix, rows, preferred_element_type=jnp.float32).astype(jnp.bfloat16)


def gather_x(mine):
    half = mine.shape[0] // 2
    left = move(mine, 1)
    right = move(mine, -1)
    top = move(left[:half], 1)
    bottom = move(right[half:], -1)
    return [mine, right, jnp.concatenate([top, bottom], axis=0), left]


def add(a, b):
    return (a.astype(jnp.float32) + b.astype(jnp.float32)).astype(jnp.bfloat16)


def reduce_x(parts):
    half = parts[0].shape[0] // 2
    top = move(parts[2][:half], 1)
    bottom = move(parts[2][half:], -1)
    one = jnp.concatenate([add(parts[1][:half], top), parts[1][half:]], axis=0)
    three = jnp.concatenate([parts[3][:half], add(parts[3][half:], bottom)], axis=0)
    from_left = move(one, 1)
    from_right = move(three, -1)
    total = parts[0].astype(jnp.float32) + from_left.astype(jnp.float32)
    return (total + from_right.astype(jnp.float32)).astype(jnp.bfloat16)


def first_kernel(idx, *refs):
    xs, gates, ups = refs[:4], refs[4:8], refs[8:12]
    g_ref, u_ref = refs[12:]
    g_ref[...] = sum(
        jnp.dot(x[...], w[...], preferred_element_type=jnp.float32) for x, w in zip(xs, gates)
    )
    u_ref[...] = sum(
        jnp.dot(x[...], w[...], preferred_element_type=jnp.float32) for x, w in zip(xs, ups)
    )


def second_kernel(idx, *refs):
    g_ref, u_ref = refs[:2]
    xs, gates, ups, downs, outs = refs[2:6], refs[6:10], refs[10:14], refs[14:22], refs[22:]
    gate = g_ref[...] + sum(
        jnp.dot(x[...], w[...], preferred_element_type=jnp.float32) for x, w in zip(xs, gates)
    )
    up = u_ref[...] + sum(
        jnp.dot(x[...], w[...], preferred_element_type=jnp.float32) for x, w in zip(xs, ups)
    )
    hidden = (gate / (1.0 + jnp.exp(-gate)) * up).astype(jnp.bfloat16)
    for down, out in zip(downs, outs):
        out[...] = jnp.dot(hidden, down[...], preferred_element_type=jnp.float32).astype(
            jnp.bfloat16
        )


def rows_spec(width):
    return pl.BlockSpec((ROW_TILE, width), lambda i, idx: (i, 0))


def first_half(idx, xs, w_gate, w_up):
    rows, width = xs[0].shape
    hidden = w_gate.shape[1]
    wspecs = [pl.BlockSpec((width, hidden), lambda i, idx, d=d: (idx[d], 0)) for d in range(4)]
    return pl.pallas_call(
        first_kernel,
        grid_spec=pltpu.PrefetchScalarGridSpec(
            num_scalar_prefetch=1,
            grid=(rows // ROW_TILE,),
            in_specs=[rows_spec(width)] * 4 + wspecs * 2,
            out_specs=[rows_spec(hidden)] * 2,
        ),
        out_shape=[jax.ShapeDtypeStruct((rows, hidden), jnp.float32)] * 2,
        compiler_params=pltpu.CompilerParams(vmem_limit_bytes=40 * 2**20),
        cost_estimate=pl.CostEstimate(
            flops=16 * rows * width * hidden, bytes_accessed=20 * 2**20, transcendentals=0
        ),
    )(idx, *xs, *[w_gate] * 4, *[w_up] * 4)


def second_half(idx, sums, xs, w_gate, w_up, w_down):
    rows, width = xs[0].shape
    hidden = w_gate.shape[1]
    wspecs = [pl.BlockSpec((width, hidden), lambda i, idx, d=d: (idx[4 + d], 0)) for d in range(4)]
    dspecs = [pl.BlockSpec((hidden, width), lambda i, idx, d=d: (0, idx[d])) for d in range(8)]
    return pl.pallas_call(
        second_kernel,
        grid_spec=pltpu.PrefetchScalarGridSpec(
            num_scalar_prefetch=1,
            grid=(rows // ROW_TILE,),
            in_specs=[rows_spec(hidden)] * 2 + [rows_spec(width)] * 4 + wspecs * 2 + dspecs,
            out_specs=[rows_spec(width)] * 8,
        ),
        out_shape=[jax.ShapeDtypeStruct((rows, width), jnp.bfloat16)] * 8,
        compiler_params=pltpu.CompilerParams(vmem_limit_bytes=48 * 2**20),
        cost_estimate=pl.CostEstimate(
            flops=32 * rows * width * hidden,
            bytes_accessed=30 * 2**20,
            transcendentals=rows * hidden,
        ),
    )(idx, *sums, *xs, *[w_gate] * 4, *[w_up] * 4, *[w_down] * 8)


def shards(tokens, slot_ids, weights, w_gate, w_up, w_down):
    n_ep = lax.axis_size("ep")
    rep = lax.axis_index("rep")
    x, zh = rep // 2, rep % 2
    steps = jnp.arange(4, dtype=jnp.int32)
    around = (x + steps) % 4 * 2
    idx = jnp.concatenate([around + zh, around + 1 - zh]).astype(jnp.int32)

    other_tokens = swap(tokens)
    row = place_rows(slot_ids, n_ep)
    slots = lax.broadcasted_iota(jnp.int32, (n_ep * PAD_PAIR, tokens.shape[0]), 0)
    pack = ((slots == row[0][None]) | (slots == row[1][None])).astype(jnp.bfloat16)
    compact = compact_matrix(n_ep)

    mine = pick(compact, exchange(pick(pack, tokens), n_ep))
    own = gather_x(mine)
    theirs = pick(compact, exchange(pick(pack, other_tokens), n_ep))
    other = gather_x(theirs)

    sums = first_half(idx, own, w_gate[0], w_up[0])
    terms = second_half(idx, sums, other, w_gate[0], w_up[0], w_down[0])

    spread = compact.T
    columns = lax.broadcasted_iota(jnp.int32, (tokens.shape[0], n_ep * PAD_PAIR), 1)
    choose = [(columns == row[k][:, None]).astype(jnp.bfloat16) for k in range(2)]

    def combine(rows):
        return sum(
            weights[:, k : k + 1] * jnp.dot(choose[k], rows, preferred_element_type=jnp.float32)
            for k in range(2)
        )

    back_other = exchange(pick(spread, reduce_x(terms[4:])), n_ep)
    sent = swap(combine(back_other).astype(jnp.bfloat16))
    back_own = exchange(pick(spread, reduce_x(terms[:4])), n_ep)
    return (combine(back_own) + sent.astype(jnp.float32)).astype(jnp.bfloat16)


def solution(mesh):
    placed = (
        P("ep", "rep"),
        P("ep", None),
        P("ep", None),
        P("ep", None, "rep"),
        P("ep", None, "rep"),
        P("ep", "rep", None),
    )
    return jax.shard_map(
        shards, mesh=mesh, in_specs=placed, out_specs=P("ep", "rep"), check_vma=False
    )
```

```python
import functools

import jax
import jax.numpy as jnp
from jax import lax
from jax.experimental import pallas as pl
from jax.experimental.pallas import tpu as pltpu
from jax.sharding import PartitionSpec as P

CAP_PAIR = 20
PAD_PAIR = 24


def move(x, by):
    return lax.ppermute(x, "rep", [(i, (i + 2 * by) % 8) for i in range(8)])


def swap(x):
    return lax.ppermute(x, "rep", [(i, i ^ 1) for i in range(8)])


def place_rows(slot_ids, n_ep):
    flat = slot_ids.T.reshape(-1)
    count = flat.shape[0]
    onehot = (flat[:, None] == jnp.arange(2 * n_ep, dtype=jnp.int32)[None, :]).astype(jnp.bfloat16)
    before = jnp.tril(jnp.ones((count, count), jnp.bfloat16), -1)
    ahead = jnp.dot(before, onehot, preferred_element_type=jnp.float32)
    position = jnp.sum(ahead * onehot.astype(jnp.float32), axis=1).astype(jnp.int32)
    odd = flat % 2
    expert = (flat // 2 - odd + n_ep) % n_ep
    row = expert * PAD_PAIR + odd * (CAP_PAIR // 2) + position
    return row.reshape(2, -1)


def exchange(rows, n_ep):
    width = rows.shape[1]
    out = lax.all_to_all(rows.reshape(n_ep, PAD_PAIR, width), "ep", 0, 0, tiled=True)
    return out.reshape(n_ep * PAD_PAIR, width)


def compact_matrix(pairs):
    r = lax.broadcasted_iota(jnp.int32, (pairs * CAP_PAIR, pairs * PAD_PAIR), 0)
    c = lax.broadcasted_iota(jnp.int32, (pairs * CAP_PAIR, pairs * PAD_PAIR), 1)
    return (r // CAP_PAIR * PAD_PAIR + r % CAP_PAIR == c).astype(jnp.bfloat16)


def pick(matrix, rows):
    return jnp.dot(matrix, rows, preferred_element_type=jnp.float32).astype(jnp.bfloat16)


def after(value, *first):
    return lax.optimization_barrier((value, *first))[0]


def ends(top, bottom):
    return move(top, 1), move(bottom, -1)


def sides(top, bottom):
    return move(bottom, 1), move(top, -1)


def add(*terms):
    return sum(t.astype(jnp.float32) for t in terms).astype(jnp.bfloat16)


def mm(a, b):
    return jnp.dot(a, b, preferred_element_type=jnp.float32)


def gate_up(pieces, start, idx, xs, wg, wu):
    sums = [list(pair) if pair else None for pair in start]
    for (block, h), x in zip(pieces, xs):
        width = x.shape[1]
        rows = pl.ds(pl.multiple_of(idx[block] * width, width), width)
        new = [mm(x[...], wg[rows, :]), mm(x[...], wu[rows, :])]
        sums[h] = [s + n for s, n in zip(sums[h], new)] if sums[h] else new
    return sums


def first_kernel(pieces, idx, *refs):
    xs, (wg, wu, g_ref, u_ref) = refs[:-4], refs[-4:]
    half = g_ref.shape[0] // 2
    for h, (gate, up) in enumerate(gate_up(pieces, [None, None], idx, xs, wg, wu)):
        g_ref[h * half : (h + 1) * half, :] = gate
        u_ref[h * half : (h + 1) * half, :] = up


def more_kernel(pieces, idx, g_in, u_in, *refs):
    xs, (wg, wu, g_ref, u_ref) = refs[:-4], refs[-4:]
    half = g_ref.shape[0] // 2
    at = [slice(h * half, (h + 1) * half) for h in range(2)]
    sums = gate_up(pieces, [(g_in[a, :], u_in[a, :]) for a in at], idx, xs, wg, wu)
    for a, (gate, up) in zip(at, sums):
        g_ref[a, :] = gate
        u_ref[a, :] = up


def second_kernel(pieces, far, idx, g_in, u_in, *refs):
    xs, (wg, wu, wd, h_ref, *outs) = refs[: len(pieces)], refs[len(pieces) :]
    half, width = xs[0].shape
    at = [slice(h * half, (h + 1) * half) for h in range(2)]
    sums = gate_up(pieces, [(g_in[a, :], u_in[a, :]) for a in at], idx, xs, wg, wu)
    columns = pl.ds(pl.multiple_of(idx[far] * width, width), width)
    for a, (gate, up), out in zip(at, sums, outs):
        hidden = (gate / (1.0 + jnp.exp(-gate)) * up).astype(jnp.bfloat16)
        h_ref[a, :] = hidden
        out[...] = mm(hidden, wd[:, columns]).astype(jnp.bfloat16)


def third_kernel(order, idx, h_ref, wd, *outs):
    half, width = outs[0].shape
    for i, b in enumerate(order):
        columns = pl.ds(pl.multiple_of(idx[b] * width, width), width)
        for h in range(2):
            hidden = h_ref[h * half : (h + 1) * half, :]
            outs[2 * i + h][...] = mm(hidden, wd[:, columns]).astype(jnp.bfloat16)


def call(body, outs, flops, *args):
    smem = pl.BlockSpec(memory_space=pltpu.SMEM)
    vmem = pl.BlockSpec(memory_space=pltpu.VMEM)
    size = sum(a.size * a.dtype.itemsize for a in (*args[1:], *outs))
    return pl.pallas_call(
        body,
        in_specs=[smem] + [vmem] * (len(args) - 1),
        out_specs=[vmem] * len(outs),
        out_shape=outs,
        compiler_params=pltpu.CompilerParams(vmem_limit_bytes=16 * 2**20),
        cost_estimate=pl.CostEstimate(flops=flops, bytes_accessed=size, transcendentals=0),
    )(*args)


def shards(tokens, slot_ids, weights, w_gate, w_up, w_down):
    n_ep = lax.axis_size("ep")
    rep = lax.axis_index("rep")
    near = [(rep + 2 * d) & 7 for d in range(4)]
    idx = jnp.stack(near + [a ^ 1 for a in near]).astype(jnp.int32)
    w_gate, w_up, w_down = w_gate[0], w_up[0], w_down[0]

    row = place_rows(slot_ids, n_ep)
    slots = lax.broadcasted_iota(jnp.int32, (n_ep * PAD_PAIR, tokens.shape[0]), 0)
    pack = ((slots == row[0][None]) | (slots == row[1][None])).astype(jnp.bfloat16)
    compact = compact_matrix(n_ep // 2)
    middle = n_ep * PAD_PAIR // 2

    arrived = exchange(pick(pack, tokens), n_ep)
    top, bottom = pick(compact, arrived[:middle]), pick(compact, arrived[middle:])
    left_top, right_bottom = ends(top, bottom)
    swap_top = swap(top)
    far_top, far_bottom = move(left_top, 1), move(right_bottom, -1)
    swap_bottom = swap(after(bottom, left_top, right_bottom))
    left_bottom, right_top = sides(after(top, left_top), after(bottom, right_bottom))

    half, width = top.shape
    hidden = w_gate.shape[1]
    unit = 4 * half * width * hidden
    bf16 = lambda *shape: jax.ShapeDtypeStruct(shape, jnp.bfloat16)
    acc = [jax.ShapeDtypeStruct((2 * half, hidden), jnp.float32)] * 2
    own = {
        (0, 0): top,
        (0, 1): bottom,
        (1, 0): right_top,
        (1, 1): right_bottom,
        (2, 0): far_top,
        (2, 1): far_bottom,
        (3, 0): left_top,
        (3, 1): left_bottom,
    }

    sums = call(
        functools.partial(first_kernel, list(own)), acc, 8 * unit, idx, *own.values(), w_gate, w_up
    )

    top = after(swap_top, left_bottom, right_top)
    left_top, right_top = move(top, 1), move(top, -1)
    bottom = after(swap_bottom, *sums, left_top, right_top)
    far_top = move(left_top, 1)
    left_bottom, right_bottom = move(bottom, 1), move(bottom, -1)
    far_bottom = move(right_bottom, -1)
    other = {
        (4, 0): top,
        (4, 1): bottom,
        (5, 0): right_top,
        (5, 1): right_bottom,
        (7, 0): left_top,
    }
    last = {(6, 0): far_top, (6, 1): far_bottom, (7, 1): left_bottom}

    sums = call(
        functools.partial(more_kernel, list(other)),
        acc,
        5 * unit,
        idx,
        *sums,
        *other.values(),
        w_gate,
        w_up,
    )
    units, *far = call(
        functools.partial(second_kernel, list(last), 6),
        [bf16(2 * half, hidden), bf16(half, width), bf16(half, width)],
        4 * unit,
        idx,
        *sums,
        *last.values(),
        w_gate,
        w_up,
        w_down,
    )
    order = (5, 7, 4, 2, 1, 3, 0)
    rest = call(
        functools.partial(third_kernel, order),
        [bf16(half, width)] * 14,
        7 * unit // 2,
        idx,
        units,
        w_down,
    )
    terms = {b: (rest[2 * i], rest[2 * i + 1]) for i, b in enumerate(order)}
    terms[6] = far

    a0, a1, a2, a3 = [terms[b] for b in (4, 5, 6, 7)]
    h0, h1, h2, h3 = [terms[b] for b in (0, 1, 2, 3)]
    far_top, far_bottom = ends(*a2)
    left_bottom, right_top = sides(a3[0], a1[1])
    left_top = move(add(a1[0], far_top), 1)
    right_bottom = move(add(a3[1], far_bottom), -1)
    home_far = ends(after(h2[0], left_bottom), after(h2[1], right_top))
    came = [
        swap(add(a0[0], left_top, right_top)),
        swap(add(a0[1], left_bottom, right_bottom)),
    ]
    left_bottom, right_top = sides(after(h3[0], right_bottom), after(h1[1], left_top))
    left_top = move(add(h1[0], home_far[0]), 1)
    right_bottom = move(add(h3[1], home_far[1]), -1)
    home = [add(h0[0], left_top, right_top), add(h0[1], left_bottom, right_bottom)]
    spread = compact.T
    total = [pick(spread, add(h, c)) for h, c in zip(home, came)]
    back = exchange(jnp.concatenate(total, axis=0), n_ep)

    columns = lax.broadcasted_iota(jnp.int32, (tokens.shape[0], n_ep * PAD_PAIR), 1)
    out = sum(
        weights[:, k : k + 1] * mm((columns == row[k][:, None]).astype(jnp.bfloat16), back)
        for k in range(2)
    )
    return out.astype(jnp.bfloat16)


def solution(mesh):
    placed = (
        P("ep", "rep"),
        P("ep", None),
        P("ep", None),
        P("ep", None, "rep"),
        P("ep", None, "rep"),
        P("ep", "rep", None),
    )
    return jax.shard_map(
        shards, mesh=mesh, in_specs=placed, out_specs=P("ep", "rep"), check_vma=False
    )
```

```python
import jax
import jax.numpy as jnp
from jax import lax
from jax.experimental import pallas as pl
from jax.experimental.pallas import tpu as pltpu
from jax.sharding import PartitionSpec as P

CAP_PAIR = 20
PAD_PAIR = 24
SPLIT = 320


def move(x, by):
    return lax.ppermute(x, "rep", [(i, (i + 2 * by) % 8) for i in range(8)])


def swap(x):
    return lax.ppermute(x, "rep", [(i, i ^ 1) for i in range(8)])


def place_rows(slot_ids, n_ep):
    flat = slot_ids.T.reshape(-1)
    count = flat.shape[0]
    onehot = (flat[:, None] == jnp.arange(2 * n_ep, dtype=jnp.int32)[None, :]).astype(jnp.bfloat16)
    before = jnp.tril(jnp.ones((count, count), jnp.bfloat16), -1)
    ahead = jnp.dot(before, onehot, preferred_element_type=jnp.float32)
    position = jnp.sum(ahead * onehot.astype(jnp.float32), axis=1).astype(jnp.int32)
    odd = flat % 2
    expert = (flat // 2 - odd + n_ep) % n_ep
    row = expert * PAD_PAIR + odd * (CAP_PAIR // 2) + position
    return row.reshape(2, -1)


def exchange(rows, n_ep):
    width = rows.shape[1]
    out = lax.all_to_all(rows.reshape(n_ep, PAD_PAIR, width), "ep", 0, 0, tiled=True)
    return out.reshape(n_ep * PAD_PAIR, width)


def compact_matrix(pairs):
    r = lax.broadcasted_iota(jnp.int32, (pairs * CAP_PAIR, pairs * PAD_PAIR), 0)
    c = lax.broadcasted_iota(jnp.int32, (pairs * CAP_PAIR, pairs * PAD_PAIR), 1)
    return (r // CAP_PAIR * PAD_PAIR + r % CAP_PAIR == c).astype(jnp.bfloat16)


def pick(matrix, rows):
    return jnp.dot(matrix, rows, preferred_element_type=jnp.float32).astype(jnp.bfloat16)


def after(value, *first):
    return lax.optimization_barrier((value, *first))[0]


class Order:
    def __init__(self):
        self.last = ()

    def __call__(self, *values):
        out = lax.optimization_barrier((*values, *self.last))[: len(values)]
        self.last = out
        return out if len(out) > 1 else out[0]


def mm(a, b):
    return jnp.dot(a, b, preferred_element_type=jnp.float32)


def add(*terms):
    return sum(t.astype(jnp.float32) for t in terms).astype(jnp.bfloat16)


def halves(x):
    half = x.shape[0] // 2
    return x[:half], x[half:]


def block(idx, i, width):
    return pl.ds(pl.multiple_of(idx[i] * width, width), width)


def first_kernel(idx, *refs):
    xs, (wg, wu, *outs) = refs[:8], refs[8:]
    width = xs[0].shape[1]
    for p in range(2):
        for m, w in enumerate((wg, wu)):
            outs[2 * p + m][...] = sum(
                mm(xs[2 * n + p][...], w[block(idx, d, width), :])
                for n, d in enumerate((0, 1, 3, 2))
            )


def second_kernel(idx, g_in, u_in, *refs):
    xs, (wg, wu, wd, h_ref, top, bottom) = refs[:5], refs[5:]
    half, width = top.shape
    sums = [g_in[...], u_in[...]]
    for m, w in enumerate((wg, wu)):
        for x, d in zip(xs[:3], (4, 5, 7)):
            sums[m] = sums[m] + mm(x[...], w[block(idx, d, width), :])
    far = [w[block(idx, 6, width), :] for w in (wg, wu)]
    for h, (x, out) in enumerate(zip(xs[3:], (top, bottom))):
        at = slice(h * half, (h + 1) * half)
        gate = sums[0][at] + mm(x[...], far[0])
        up = sums[1][at] + mm(x[...], far[1])
        hidden = (gate / (1.0 + jnp.exp(-gate)) * up).astype(jnp.bfloat16)
        h_ref[at, :] = hidden
        out[...] = mm(hidden, wd[:, block(idx, 6, width)]).astype(jnp.bfloat16)


REST = (5, 7, 4, 2, 1, 3, 0)


def third_kernel(idx, h_ref, wd, *outs):
    hidden, width = h_ref[...], outs[0].shape[1]
    for i, out in zip(REST, outs):
        out[...] = mm(hidden, wd[:, block(idx, i, width)]).astype(jnp.bfloat16)


def fold_kernel(one, three, top, bottom, one_out, three_out):
    half = top.shape[0]
    one_out[:half, :] = add(one[:half, :], top[...])
    one_out[half:, :] = one[half:, :]
    three_out[:half, :] = three[:half, :]
    three_out[half:, :] = add(three[half:, :], bottom[...])


def call(body, outs, flops, *args):
    smem = pl.BlockSpec(memory_space=pltpu.SMEM)
    vmem = pl.BlockSpec(memory_space=pltpu.VMEM)
    size = sum(a.size * a.dtype.itemsize for a in (*args, *outs))
    return pl.pallas_call(
        body,
        in_specs=[smem if a.ndim == 1 else vmem for a in args],
        out_specs=[vmem] * len(outs),
        out_shape=outs,
        compiler_params=pltpu.CompilerParams(vmem_limit_bytes=16 * 2**20),
        cost_estimate=pl.CostEstimate(flops=flops, bytes_accessed=size, transcendentals=0),
    )(*args)


def bf16(*shape):
    return jax.ShapeDtypeStruct(shape, jnp.bfloat16)


def fold(*terms):
    return call(fold_kernel, [bf16(*terms[0].shape)] * 2, terms[0].size, *terms)


def near(x):
    return move(x, 1), move(x, -1)


def far(left, right):
    return move(halves(left)[0], 1), move(halves(right)[1], -1)


def shards(tokens, slot_ids, weights, w_gate, w_up, w_down):
    n_ep = lax.axis_size("ep")
    rep = lax.axis_index("rep")
    around = [(rep + 2 * d) & 7 for d in range(4)]
    idx = jnp.stack(around + [a ^ 1 for a in around]).astype(jnp.int32)
    w_gate, w_up, w_down = w_gate[0], w_up[0], w_down[0]

    row = place_rows(slot_ids, n_ep)
    slots = lax.broadcasted_iota(jnp.int32, (n_ep * PAD_PAIR, tokens.shape[0]), 0)
    pack = ((slots == row[0][None]) | (slots == row[1][None])).astype(jnp.bfloat16)
    compact = compact_matrix(n_ep)

    arrived = exchange(pick(pack, tokens), n_ep)
    top, bottom = pick(compact[:SPLIT], arrived), pick(compact[SPLIT:], arrived)
    width, hidden = tokens.shape[1], w_gate.shape[1]
    order = Order()

    def units(sums, *xs):
        rows = xs[0].shape[0]
        return call(
            second_kernel,
            [bf16(rows, hidden), bf16(rows // 2, width), bf16(rows // 2, width)],
            18 * rows * width * hidden,
            idx,
            *sums,
            *xs,
            w_gate,
            w_up,
            w_down,
        )

    def terms(hid):
        rows = hid.shape[0]
        return call(
            third_kernel,
            [bf16(rows, width)] * len(REST),
            14 * rows * width * hidden,
            idx,
            hid,
            w_down,
        )

    lt, rb = move(top, 1), move(bottom, -1)
    swap1 = swap(top)
    ft, fb = move(lt, 1), move(rb, -1)
    swap2 = swap(after(bottom, lt, rb))
    lb, rt = move(after(bottom, rb), 1), move(after(top, lt), -1)
    acc = lambda x: [jax.ShapeDtypeStruct((x.shape[0], hidden), jnp.float32)] * 2
    sums = call(
        first_kernel,
        acc(top) + acc(bottom),
        16 * compact.shape[0] * width * hidden,
        idx,
        *(top, bottom, rt, rb, lt, lb, ft, fb),
        w_gate,
        w_up,
    )
    o1 = after(swap1, lb, rt)
    l1, r1 = near(o1)
    f1a, f1b = far(l1, r1)
    o2 = after(swap2, *sums, l1, r1)
    l2, r2 = near(o2)
    f1a, f1b = order(f1a, f1b)

    hid, ga, gb = order(*units(sums[:2], o1, r1, l1, f1a, f1b))
    ga, gb = move(ga, 1), move(gb, -1)
    t5, t7, t4, t2, t1, t3, t0 = terms(hid)
    l2, r2 = order(l2, r2)
    f2a, f2b = far(l2, r2)
    ga, gb = order(ga, gb)
    one, three = fold(t5, t7, ga, gb)
    ol, orr = move(one, 1), move(three, -1)
    f2a, f2b = order(f2a, f2b)
    hid, ga, gb = order(*units(sums[2:], o2, r2, l2, f2a, f2b))
    ga, gb = move(ga, 1), move(gb, -1)
    b5, b7, b4, b2, b1, b3, b0 = terms(hid)
    ol, orr = order(ol, orr)
    came1 = swap(add(t4, ol, orr))
    ga, gb = order(ga, gb)
    one, three = fold(b5, b7, ga, gb)
    ol, orr = move(one, 1), move(three, -1)

    ft, fb = move(lax.optimization_barrier((t2, ga))[0], 1), move(b2, -1)
    ol, orr = order(ol, orr)
    came2 = swap(add(b4, ol, orr))
    lb = move(lax.optimization_barrier((b1, ol))[0], 1)
    rt = move(lax.optimization_barrier((t3, orr))[0], -1)
    came1 = order(came1)
    ft, fb = order(ft, fb)
    lt, rb = move(add(t1, ft), 1), move(add(b3, fb), -1)
    lb, rt = order(lb, rt)
    lt, rb = order(lt, rb)
    total = jnp.concatenate([add(t0, lt, rt, came1), add(b0, lb, rb, came2)], axis=0)
    back = exchange(pick(compact.T, total), n_ep)

    columns = lax.broadcasted_iota(jnp.int32, (tokens.shape[0], n_ep * PAD_PAIR), 1)
    out = sum(
        weights[:, k : k + 1] * mm((columns == row[k][:, None]).astype(jnp.bfloat16), back)
        for k in range(2)
    )
    return out.astype(jnp.bfloat16)


def solution(mesh):
    placed = (
        P("ep", "rep"),
        P("ep", None),
        P("ep", None),
        P("ep", None, "rep"),
        P("ep", None, "rep"),
        P("ep", "rep", None),
    )
    return jax.shard_map(
        shards, mesh=mesh, in_specs=placed, out_specs=P("ep", "rep"), check_vma=False
    )
```

```python
import jax
import jax.numpy as jnp
from jax import lax
from jax.experimental import pallas as pl
from jax.experimental.pallas import tpu as pltpu
from jax.sharding import PartitionSpec as P

CAP_PAIR = 20
PAD_PAIR = 24
ROW_TILE = 160
FOLD_TILE = 32


def move(x, by):
    return lax.ppermute(x, "rep", [(i, (i + 2 * by) % 8) for i in range(8)])


def swap(x):
    return lax.ppermute(x, "rep", [(i, i ^ 1) for i in range(8)])


def place_rows(slot_ids, n_ep):
    flat = slot_ids.T.reshape(-1)
    count = flat.shape[0]
    onehot = (flat[:, None] == jnp.arange(2 * n_ep, dtype=jnp.int32)[None, :]).astype(jnp.bfloat16)
    before = jnp.tril(jnp.ones((count, count), jnp.bfloat16), -1)
    ahead = jnp.dot(before, onehot, preferred_element_type=jnp.float32)
    position = jnp.sum(ahead * onehot.astype(jnp.float32), axis=1).astype(jnp.int32)
    odd = flat % 2
    expert = (flat // 2 - odd + n_ep) % n_ep
    row = expert * PAD_PAIR + odd * (CAP_PAIR // 2) + position
    return row.reshape(2, -1)


def exchange(rows, n_ep):
    width = rows.shape[1]
    out = lax.all_to_all(rows.reshape(n_ep, PAD_PAIR, width), "ep", 0, 0, tiled=True)
    return out.reshape(n_ep * PAD_PAIR, width)


def compact_matrix(pairs):
    r = lax.broadcasted_iota(jnp.int32, (pairs * CAP_PAIR, pairs * PAD_PAIR), 0)
    c = lax.broadcasted_iota(jnp.int32, (pairs * CAP_PAIR, pairs * PAD_PAIR), 1)
    return (r // CAP_PAIR * PAD_PAIR + r % CAP_PAIR == c).astype(jnp.bfloat16)


def pick(matrix, rows):
    return jnp.dot(matrix, rows, preferred_element_type=jnp.float32).astype(jnp.bfloat16)


def after(value, *first):
    return lax.optimization_barrier((value, *first))[0]


class Order:
    def __init__(self):
        self.last = ()

    def __call__(self, *values):
        out = lax.optimization_barrier((*values, *self.last))[: len(values)]
        self.last = out
        return out if len(out) > 1 else out[0]


def mm(a, b):
    return jnp.dot(a, b, preferred_element_type=jnp.float32)


def add(*terms):
    return sum(t.astype(jnp.float32) for t in terms).astype(jnp.bfloat16)


def halves(x):
    half = x.shape[0] // 2
    return x[:half], x[half:]


def block(idx, i, width):
    return pl.ds(pl.multiple_of(idx[i] * width, width), width)


def first_kernel(idx, *refs):
    xs, (wg, wu, *outs) = refs[:8], refs[8:]
    rows, width = xs[0].shape

    @pl.loop(0, rows // ROW_TILE)
    def _(i):
        at = pl.ds(pl.multiple_of(i * ROW_TILE, ROW_TILE), ROW_TILE)
        for p in range(2):
            for m, w in enumerate((wg, wu)):
                outs[2 * p + m][at, :] = sum(
                    mm(xs[2 * n + p][at, :], w[block(idx, d, width), :])
                    for n, d in enumerate((0, 1, 3, 2))
                )


def second_kernel(idx, g_in, u_in, *refs):
    xs, (wg, wu, wd, h_ref, top, bottom, *sums) = refs[:5], refs[5:]
    half, width = top.shape

    @pl.loop(0, 2)
    def _(i):
        at = pl.ds(pl.multiple_of(i * half, half), half)
        for w, start, total in zip((wg, wu), (g_in, u_in), sums):
            total[at, :] = start[at, :] + sum(
                mm(x[at, :], w[block(idx, d, width), :]) for x, d in zip(xs[:3], (4, 5, 7))
            )

    for h, (x, out) in enumerate(zip(xs[3:], (top, bottom))):
        at = slice(h * half, (h + 1) * half)
        gate, up = [
            total[at, :] + mm(x[...], w[block(idx, 6, width), :])
            for w, total in zip((wg, wu), sums)
        ]
        hidden = (gate / (1.0 + jnp.exp(-gate)) * up).astype(jnp.bfloat16)
        h_ref[at, :] = hidden
        out[...] = mm(hidden, wd[:, block(idx, 6, width)]).astype(jnp.bfloat16)


REST = (5, 7, 4, 2, 1, 3, 0)


def third_kernel(idx, h_ref, wd, *outs):
    rows, width = outs[0].shape

    @pl.loop(0, rows // ROW_TILE)
    def _(j):
        at = pl.ds(pl.multiple_of(j * ROW_TILE, ROW_TILE), ROW_TILE)
        hidden = h_ref[at, :]
        for i, out in zip(REST, outs):
            out[at, :] = mm(hidden, wd[:, block(idx, i, width)]).astype(jnp.bfloat16)


def fold_kernel(one, three, top, bottom, one_out, three_out):
    half = top.shape[0]

    @pl.loop(0, half // FOLD_TILE)
    def _(i):
        upper = pl.ds(pl.multiple_of(i * FOLD_TILE, FOLD_TILE), FOLD_TILE)
        lower = pl.ds(pl.multiple_of(half + i * FOLD_TILE, FOLD_TILE), FOLD_TILE)
        one_out[upper, :] = add(one[upper, :], top[upper, :])
        one_out[lower, :] = one[lower, :]
        three_out[upper, :] = three[upper, :]
        three_out[lower, :] = add(three[lower, :], bottom[upper, :])


def call(body, outs, flops, *args, scratch=()):
    smem = pl.BlockSpec(memory_space=pltpu.SMEM)
    vmem = pl.BlockSpec(memory_space=pltpu.VMEM)
    size = sum(a.size * a.dtype.itemsize for a in (*args, *outs))
    return pl.pallas_call(
        body,
        in_specs=[smem if a.ndim == 1 else vmem for a in args],
        out_specs=[vmem] * len(outs),
        out_shape=outs,
        scratch_shapes=scratch,
        compiler_params=pltpu.CompilerParams(vmem_limit_bytes=16 * 2**20),
        cost_estimate=pl.CostEstimate(flops=flops, bytes_accessed=size, transcendentals=0),
    )(*args)


def bf16(*shape):
    return jax.ShapeDtypeStruct(shape, jnp.bfloat16)


def fold(*terms):
    return call(fold_kernel, [bf16(*terms[0].shape)] * 2, terms[0].size, *terms)


def near(x):
    return move(x, 1), move(x, -1)


def far(left, right):
    return move(halves(left)[0], 1), move(halves(right)[1], -1)


def shards(tokens, slot_ids, weights, w_gate, w_up, w_down):
    n_ep = lax.axis_size("ep")
    rep = lax.axis_index("rep")
    around = [(rep + 2 * d) & 7 for d in range(4)]
    idx = jnp.stack(around + [a ^ 1 for a in around]).astype(jnp.int32)
    w_gate, w_up, w_down = w_gate[0], w_up[0], w_down[0]

    row = place_rows(slot_ids, n_ep)
    slots = lax.broadcasted_iota(jnp.int32, (n_ep * PAD_PAIR, tokens.shape[0]), 0)
    pack = ((slots == row[0][None]) | (slots == row[1][None])).astype(jnp.bfloat16)
    compact = compact_matrix(n_ep // 2)
    middle = n_ep * PAD_PAIR // 2

    arrived = exchange(pick(pack, tokens), n_ep)
    top, bottom = pick(compact, arrived[:middle]), pick(compact, arrived[middle:])
    width, hidden = tokens.shape[1], w_gate.shape[1]
    order = Order()

    def units(sums, *xs):
        rows = xs[0].shape[0]
        return call(
            second_kernel,
            [bf16(rows, hidden), bf16(rows // 2, width), bf16(rows // 2, width)],
            18 * rows * width * hidden,
            idx,
            *sums,
            *xs,
            w_gate,
            w_up,
            w_down,
            scratch=[pltpu.VMEM((rows, hidden), jnp.float32)] * 2,
        )

    def terms(hid):
        rows = hid.shape[0]
        return call(
            third_kernel,
            [bf16(rows, width)] * len(REST),
            14 * rows * width * hidden,
            idx,
            hid,
            w_down,
        )

    lt, rb = move(top, 1), move(bottom, -1)
    swap1 = swap(top)
    ft, fb = move(lt, 1), move(rb, -1)
    swap2 = swap(after(bottom, lt, rb))
    lb, rt = move(after(bottom, rb), 1), move(after(top, lt), -1)
    acc = lambda x: [jax.ShapeDtypeStruct((x.shape[0], hidden), jnp.float32)] * 2
    sums = call(
        first_kernel,
        acc(top) + acc(bottom),
        32 * top.shape[0] * width * hidden,
        idx,
        *(top, bottom, rt, rb, lt, lb, ft, fb),
        w_gate,
        w_up,
    )
    o1 = after(swap1, lb, rt)
    l1, r1 = near(o1)
    f1a, f1b = far(l1, r1)
    o2 = after(swap2, *sums, l1, r1)
    l2, r2 = near(o2)
    f1a, f1b = order(f1a, f1b)

    hid, ga, gb = order(*units(sums[:2], o1, r1, l1, f1a, f1b))
    ga, gb = move(ga, 1), move(gb, -1)
    t5, t7, t4, t2, t1, t3, t0 = terms(hid)
    l2, r2 = order(l2, r2)
    f2a, f2b = far(l2, r2)
    ga, gb = order(ga, gb)
    one, three = fold(t5, t7, ga, gb)
    ol, orr = move(one, 1), move(three, -1)
    f2a, f2b = order(f2a, f2b)
    hid, ga, gb = order(*units(sums[2:], o2, r2, l2, f2a, f2b))
    ga, gb = move(ga, 1), move(gb, -1)
    b5, b7, b4, b2, b1, b3, b0 = terms(hid)
    ol, orr = order(ol, orr)
    came1 = swap(add(t4, ol, orr))
    ga, gb = order(ga, gb)
    one, three = fold(b5, b7, ga, gb)
    ol, orr = move(one, 1), move(three, -1)

    ft, fb = move(lax.optimization_barrier((t2, ga))[0], 1), move(b2, -1)
    ol, orr = order(ol, orr)
    came2 = swap(add(b4, ol, orr))
    lb = move(lax.optimization_barrier((b1, ol))[0], 1)
    rt = move(lax.optimization_barrier((t3, orr))[0], -1)
    came1 = order(came1)
    ft, fb = order(ft, fb)
    lt, rb = move(add(t1, ft), 1), move(add(b3, fb), -1)
    lb, rt = order(lb, rt)
    lt, rb = order(lt, rb)
    spread = compact.T
    total = [pick(spread, add(t0, lt, rt, came1)), pick(spread, add(b0, lb, rb, came2))]
    back = exchange(jnp.concatenate(total, axis=0), n_ep)

    columns = lax.broadcasted_iota(jnp.int32, (tokens.shape[0], n_ep * PAD_PAIR), 1)
    out = sum(
        weights[:, k : k + 1] * mm((columns == row[k][:, None]).astype(jnp.bfloat16), back)
        for k in range(2)
    )
    return out.astype(jnp.bfloat16)


def solution(mesh):
    placed = (
        P("ep", "rep"),
        P("ep", None),
        P("ep", None),
        P("ep", None, "rep"),
        P("ep", None, "rep"),
        P("ep", "rep", None),
    )
    return jax.shard_map(
        shards, mesh=mesh, in_specs=placed, out_specs=P("ep", "rep"), check_vma=False
    )
```

```python
import jax
import jax.numpy as jnp
from jax import lax
from jax.experimental import pallas as pl
from jax.experimental.pallas import tpu as pltpu
from jax.sharding import PartitionSpec as P

CAP_PAIR = 20
PAD_PAIR = 24
ROW_TILE = 160
FOLD_TILE = 32


def move(x, by):
    return lax.ppermute(x, "rep", [(i, (i + 2 * by) % 8) for i in range(8)])


def swap(x):
    return lax.ppermute(x, "rep", [(i, i ^ 1) for i in range(8)])


def place_rows(slot_ids, n_ep):
    flat = slot_ids.T.reshape(-1)
    count = flat.shape[0]
    onehot = (flat[:, None] == jnp.arange(2 * n_ep, dtype=jnp.int32)[None, :]).astype(jnp.bfloat16)
    before = jnp.tril(jnp.ones((count, count), jnp.bfloat16), -1)
    ahead = jnp.dot(before, onehot, preferred_element_type=jnp.float32)
    position = jnp.sum(ahead * onehot.astype(jnp.float32), axis=1).astype(jnp.int32)
    odd = flat % 2
    expert = (flat // 2 - odd + n_ep) % n_ep
    row = expert * PAD_PAIR + odd * (CAP_PAIR // 2) + position
    return row.reshape(2, -1)


def exchange(rows, n_ep):
    width = rows.shape[1]
    out = lax.all_to_all(rows.reshape(n_ep, PAD_PAIR, width), "ep", 0, 0, tiled=True)
    return out.reshape(n_ep * PAD_PAIR, width)


def compact_matrix(pairs):
    r = lax.broadcasted_iota(jnp.int32, (pairs * CAP_PAIR, pairs * PAD_PAIR), 0)
    c = lax.broadcasted_iota(jnp.int32, (pairs * CAP_PAIR, pairs * PAD_PAIR), 1)
    return (r // CAP_PAIR * PAD_PAIR + r % CAP_PAIR == c).astype(jnp.bfloat16)


def pick(matrix, rows):
    return jnp.dot(matrix, rows, preferred_element_type=jnp.float32).astype(jnp.bfloat16)


def after(value, *first):
    return lax.optimization_barrier((value, *first))[0]


class Order:
    def __init__(self):
        self.last = ()

    def __call__(self, *values):
        out = lax.optimization_barrier((*values, *self.last))[: len(values)]
        self.last = out
        return out if len(out) > 1 else out[0]


def mm(a, b):
    return jnp.dot(a, b, preferred_element_type=jnp.float32)


def add(*terms):
    return sum(t.astype(jnp.float32) for t in terms).astype(jnp.bfloat16)


def halves(x):
    half = x.shape[0] // 2
    return x[:half], x[half:]


def block(idx, i, width):
    return pl.ds(pl.multiple_of(idx[i] * width, width), width)


def first_kernel(idx, *refs):
    xs, (wg, wu, *outs) = refs[:8], refs[8:]
    rows, width = xs[0].shape

    @pl.loop(0, rows // ROW_TILE)
    def _(i):
        at = pl.ds(pl.multiple_of(i * ROW_TILE, ROW_TILE), ROW_TILE)
        for p in range(2):
            for m, w in enumerate((wg, wu)):
                outs[2 * p + m][at, :] = sum(
                    mm(xs[2 * n + p][at, :], w[block(idx, d, width), :])
                    for n, d in enumerate((0, 1, 3, 2))
                )


def second_kernel(idx, g_in, u_in, *refs):
    xs, (wg, wu, wd, h_ref, top, bottom, *sums) = refs[:5], refs[5:]
    half, width = top.shape

    @pl.loop(0, 2)
    def _(i):
        at = pl.ds(pl.multiple_of(i * half, half), half)
        for w, start, total in zip((wg, wu), (g_in, u_in), sums):
            total[at, :] = start[at, :] + sum(
                mm(x[at, :], w[block(idx, d, width), :]) for x, d in zip(xs[:3], (4, 5, 7))
            )

    for h, (x, out) in enumerate(zip(xs[3:], (top, bottom))):
        at = slice(h * half, (h + 1) * half)
        gate, up = [
            total[at, :] + mm(x[...], w[block(idx, 6, width), :])
            for w, total in zip((wg, wu), sums)
        ]
        hidden = (gate / (1.0 + jnp.exp(-gate)) * up).astype(jnp.bfloat16)
        h_ref[at, :] = hidden
        out[...] = mm(hidden, wd[:, block(idx, 6, width)]).astype(jnp.bfloat16)


REST = (5, 7, 4, 2, 1, 3, 0)


def third_kernel(idx, h_ref, wd, *outs):
    rows, width = outs[0].shape

    @pl.loop(0, rows // ROW_TILE)
    def _(j):
        at = pl.ds(pl.multiple_of(j * ROW_TILE, ROW_TILE), ROW_TILE)
        hidden = h_ref[at, :]
        for i, out in zip(REST, outs):
            out[at, :] = mm(hidden, wd[:, block(idx, i, width)]).astype(jnp.bfloat16)


def fold_kernel(one, three, top, bottom, one_out, three_out):
    half = top.shape[0]

    @pl.loop(0, half // FOLD_TILE)
    def _(i):
        upper = pl.ds(pl.multiple_of(i * FOLD_TILE, FOLD_TILE), FOLD_TILE)
        lower = pl.ds(pl.multiple_of(half + i * FOLD_TILE, FOLD_TILE), FOLD_TILE)
        one_out[upper, :] = add(one[upper, :], top[upper, :])
        one_out[lower, :] = one[lower, :]
        three_out[upper, :] = three[upper, :]
        three_out[lower, :] = add(three[lower, :], bottom[upper, :])


def call(body, outs, flops, *args, scratch=()):
    smem = pl.BlockSpec(memory_space=pltpu.SMEM)
    vmem = pl.BlockSpec(memory_space=pltpu.VMEM)
    size = sum(a.size * a.dtype.itemsize for a in (*args, *outs))
    return pl.pallas_call(
        body,
        in_specs=[smem if a.ndim == 1 else vmem for a in args],
        out_specs=[vmem] * len(outs),
        out_shape=outs,
        scratch_shapes=scratch,
        compiler_params=pltpu.CompilerParams(vmem_limit_bytes=16 * 2**20),
        cost_estimate=pl.CostEstimate(flops=flops, bytes_accessed=size, transcendentals=0),
    )(*args)


def bf16(*shape):
    return jax.ShapeDtypeStruct(shape, jnp.bfloat16)


def fold(*terms):
    return call(fold_kernel, [bf16(*terms[0].shape)] * 2, terms[0].size, *terms)


def near(x):
    return move(x, 1), move(x, -1)


def far(left, right):
    return move(halves(left)[0], 1), move(halves(right)[1], -1)


def shards(tokens, slot_ids, weights, w_gate, w_up, w_down):
    n_ep = lax.axis_size("ep")
    rep = lax.axis_index("rep")
    around = [(rep + 2 * d) & 7 for d in range(4)]
    idx = jnp.stack(around + [a ^ 1 for a in around]).astype(jnp.int32)
    w_gate, w_up, w_down = w_gate[0], w_up[0], w_down[0]

    row = place_rows(slot_ids, n_ep)
    slots = lax.broadcasted_iota(jnp.int32, (n_ep * PAD_PAIR, tokens.shape[0]), 0)
    pack = ((slots == row[0][None]) | (slots == row[1][None])).astype(jnp.bfloat16)
    compact = compact_matrix(n_ep // 2)
    middle = n_ep * PAD_PAIR // 2

    arrived = exchange(pick(pack, tokens), n_ep)
    top, bottom = pick(compact, arrived[:middle]), pick(compact, arrived[middle:])
    width, hidden = tokens.shape[1], w_gate.shape[1]
    order = Order()

    def units(sums, *xs):
        rows = xs[0].shape[0]
        return call(
            second_kernel,
            [bf16(rows, hidden), bf16(rows // 2, width), bf16(rows // 2, width)],
            18 * rows * width * hidden,
            idx,
            *sums,
            *xs,
            w_gate,
            w_up,
            w_down,
            scratch=[pltpu.VMEM((rows, hidden), jnp.float32)] * 2,
        )

    def terms(hid):
        rows = hid.shape[0]
        return call(
            third_kernel,
            [bf16(rows, width)] * len(REST),
            14 * rows * width * hidden,
            idx,
            hid,
            w_down,
        )

    lt, rb = move(top, 1), move(after(bottom, top), -1)
    swap1 = swap(top)
    ft, fb = move(lt, 1), move(rb, -1)
    swap2 = swap(after(bottom, lt, rb))
    lb, rt = move(after(bottom, rb), 1), move(after(top, lt), -1)
    acc = lambda x: [jax.ShapeDtypeStruct((x.shape[0], hidden), jnp.float32)] * 2
    sums = call(
        first_kernel,
        acc(top) + acc(bottom),
        32 * top.shape[0] * width * hidden,
        idx,
        *(top, bottom, rt, rb, lt, lb, ft, fb),
        w_gate,
        w_up,
    )
    o1 = after(swap1, lb, rt)
    l1, r1 = near(o1)
    f1a, f1b = far(l1, r1)
    o2 = after(swap2, *sums, l1, r1)
    l2, r2 = near(o2)
    f1a, f1b = order(f1a, f1b)

    hid, ga, gb = order(*units(sums[:2], o1, r1, l1, f1a, f1b))
    ga, gb = move(ga, 1), move(gb, -1)
    t5, t7, t4, t2, t1, t3, t0 = terms(hid)
    l2, r2 = order(l2, r2)
    f2a, f2b = far(l2, r2)
    ga, gb = order(ga, gb)
    one, three = fold(t5, t7, ga, gb)
    ol, orr = move(one, 1), move(three, -1)
    f2a, f2b = order(f2a, f2b)
    hid, ga, gb = order(*units(sums[2:], o2, r2, l2, f2a, f2b))
    ga, gb = move(ga, 1), move(gb, -1)
    b5, b7, b4, b2, b1, b3, b0 = terms(hid)
    ol, orr = order(ol, orr)
    came1 = swap(add(t4, ol, orr))
    ga, gb = order(ga, gb)
    one, three = fold(b5, b7, ga, gb)
    ol, orr = move(one, 1), move(three, -1)

    ft, fb = move(lax.optimization_barrier((t2, ga))[0], 1), move(b2, -1)
    ol, orr = order(ol, orr)
    came2 = swap(add(b4, ol, orr))
    lb = move(lax.optimization_barrier((b1, ol))[0], 1)
    rt = move(lax.optimization_barrier((t3, orr))[0], -1)
    came1 = order(came1)
    ft, fb = order(ft, fb)
    lt, rb = move(add(t1, ft), 1), move(add(b3, fb), -1)
    lb, rt = order(lb, rt)
    lt, rb = order(lt, rb)
    spread = compact.T
    total = [pick(spread, add(t0, lt, rt, came1)), pick(spread, add(b0, lb, rb, came2))]
    back = exchange(jnp.concatenate(total, axis=0), n_ep)

    count = tokens.shape[0]
    columns = lax.broadcasted_iota(jnp.int32, (2 * count, n_ep * PAD_PAIR), 1)
    choose = (columns == row.reshape(-1)[:, None]).astype(jnp.bfloat16)
    chosen = mm(choose, back)
    out = weights[:, :1] * chosen[:count] + weights[:, 1:] * chosen[count:]
    return out.astype(jnp.bfloat16)


def solution(mesh):
    placed = (
        P("ep", "rep"),
        P("ep", None),
        P("ep", None),
        P("ep", None, "rep"),
        P("ep", None, "rep"),
        P("ep", "rep", None),
    )
    return jax.shard_map(
        shards, mesh=mesh, in_specs=placed, out_specs=P("ep", "rep"), check_vma=False
    )
```
